32 devices in a mesh: grp: 2 (over y), seq: 8 (over z, core), qry: 2 (over x), fac: 1.
Axes of the slice: x: 2, y: 2, z: 4, core: 2. Of those that a mesh axis runs over, the one named last changes fastest.
Arguments:
- activations: bfloat16 [13824, 4096], P(('qry', 'fac'), ('grp', 'seq')), parts along dimension 1, may hold values from -6 to 6
- gradients: bfloat16 [5120, 4096], P(('qry', 'fac'), ('grp', 'seq')), parts along dimension 1, may hold values from -6 to 6
- input_basis: bfloat16 [24, 576, 576], P(('qry', 'fac')), may hold values from -0.25 to 0.25
- output_basis: bfloat16 [8, 640, 640], P(('qry', 'fac')), may hold values from -0.25 to 0.25
- query_left: bfloat16 [8, 32, 5120], P('seq', None, ('qry', 'fac')), may hold values from -0.078125 to 0.078125
- query_right: bfloat16 [8, 32, 13824], P('seq', None, ('qry', 'fac')), may hold values from -0.0012207031 to 0.0012207031
- lengths: int32 [128], P('grp'), parts along dimension 0, may hold values from 1 to 249, as said below
- sequence_ids: int32 [128], P('grp'), parts along dimension 0, may hold values from 0 to 63, each once
Outputs:
- scores: float32 [128, 8], P(('grp', 'seq', 'qry', 'fac')), parts along dimension 0
The draws below stay inside these ranges and needn't reach their ends.
There are 2 independent parts, one for each index of `grp`. The reference program is written for one: setup_inputs(seed, part) draws one part's arguments, and reference() takes and returns one part's arrays. A program takes and returns all parts, laid end to end along the dimension named above; an argument that names none is the same for every part. Nothing has to cross between parts.
Inputs may be any that keep to these rules, and one draw needn't show every extreme that they name: The sequences at positions 8 * k to 8 * k + 7 lie on the k-th device along seq, packed in position order from its first slot. Their lengths sum to at most 256 on every device; exactly 4 devices hold more than 192 tokens, one of them exactly 256, and one other device holds exactly 192. `sequence_ids`: each id appears once.
All inputs are finite; a program needn't handle non-finite values.
Results may differ from the reference program's by a relative error of at most 0.0041.
Values may be sent and summed in bfloat16 or wider, within the bound.
A program may use at most 64 MiB of HBM per device.

```python
import jax
import jax.numpy as jnp
from jax import lax

D = 5120
FF = 13824
BA = 576
BG = 640
R = 32
SPD = 8
KEEP = 192
CAP = 256
HEAVY = 4
NSEQ = 64
NTOK = 2048
NQ = 8
N_SEQ = 8


def draw_lengths(key, part):
    key = jax.random.fold_in(key, 11)
    rank_key, heavy_key, light_key, split_key = jax.random.split(key, 4)
    ranking = jax.random.permutation(rank_key, N_SEQ)
    heavy_loads = jax.random.randint(heavy_key, (N_SEQ,), KEEP + 1, CAP + 1)
    light_loads = jax.random.randint(light_key, (N_SEQ,), max(SPD, KEEP // 2), KEEP + 1)
    device_loads = jnp.where(ranking < HEAVY, heavy_loads, light_loads)
    device_loads = jnp.where(ranking == 0, CAP, device_loads)
    device_loads = jnp.where(ranking == HEAVY, KEEP, device_loads)
    shares = jax.random.randint(split_key, (N_SEQ, SPD), 1, 9)
    spread_total = device_loads - SPD
    seq_parts = 1 + spread_total[:, None] * shares // jnp.sum(shares, axis=1, keepdims=True)
    seq_parts = jnp.where((ranking == 0)[:, None], 1, seq_parts)
    last_part = device_loads - jnp.sum(seq_parts[:, :-1], axis=1)
    seq_parts = jnp.concatenate([seq_parts[:, :-1], last_part[:, None]], axis=1)
    return seq_parts.reshape(N_SEQ * SPD).astype(jnp.int32)


def levels(key, dims, shards, least, high):
    def one(axis_at, blocks):
        steps = jax.random.uniform(jax.random.fold_in(jax.random.fold_in(key, 6), axis_at), (blocks,), jnp.float32, least / len(shards), high / len(shards))
        return jnp.repeat(jnp.exp(steps), dims[axis_at] // blocks).reshape((-1,) + (1,) * (len(dims) - axis_at - 1))

    factor_of = one(*shards[0])
    for cut in shards[1:]:
        factor_of = factor_of * one(*cut)
    return factor_of


def noise(stream_key, dims, deviation, most, cuts=(), held_as=jnp.bfloat16):
    drawn = jax.random.normal(stream_key, dims, jnp.float32) * deviation
    if len(cuts) > 0:
        drawn = levels(stream_key, dims, cuts, -0.22, 0.18) * drawn
    return jnp.clip(drawn, min=-most, max=most).astype(held_as)


def setup_inputs(seed: int = 0, part: int = 0) -> dict:
    key_of = jax.random.split(jax.random.key(seed), 9)
    own_keys = jax.random.split(jax.random.fold_in(key_of[8], part), 9)
    activations = noise(own_keys[0], (FF, NTOK), 1.0, 6.0, ((0, 2), (1, 8)))
    gradients = noise(own_keys[1], (D, NTOK), 1.0, 6.0, ((0, 2), (1, 8)))
    input_basis = noise(key_of[2], (FF // BA, BA, BA), BA ** -0.5, 0.25, ((0, 2),))
    output_basis = noise(key_of[3], (D // BG, BG, BG), BG ** -0.5, 0.25, ((0, 2),))
    query_left = noise(key_of[4], (NQ, R, D), D ** -0.5, 0.078125, ((0, 8), (2, 2)))
    query_right = noise(key_of[5], (NQ, R, FF), (64 * R * FF) ** -0.5, 0.0012207031, ((0, 8), (2, 2)))
    lengths = draw_lengths(jax.random.fold_in(jax.random.fold_in(key_of[8], part), 71), part)
    sequence_ids = jax.random.permutation(own_keys[7], NSEQ).astype(jnp.int32)
    return {"activations": activations, "gradients": gradients, "input_basis": input_basis, "output_basis": output_basis, "query_left": query_left, "query_right": query_right, "lengths": lengths, "sequence_ids": sequence_ids}


def project(eigen_basis, feature_rows):
    blocks = eigen_basis.shape[0]
    block_width = eigen_basis.shape[1]
    columns = feature_rows.shape[1]
    shaped = feature_rows.reshape(blocks, block_width, columns).astype(jnp.float32)
    mapped = jnp.einsum("bij,bin->bjn", eigen_basis.astype(jnp.float32), shaped)
    return mapped.reshape(blocks * block_width, columns).astype(jnp.bfloat16)


def reference(activations, gradients, input_basis, output_basis, query_left, query_right, lengths, sequence_ids):
    device_count = lengths.shape[0] // SPD
    capacity = activations.shape[1] // device_count
    query_count = query_left.shape[0]
    rank_count = query_left.shape[1]
    left_flat = query_left.reshape(query_count * rank_count, D).astype(jnp.float32)
    right_flat = query_right.reshape(query_count * rank_count, FF).astype(jnp.float32)
    seq_ends = jnp.cumsum(lengths.reshape(device_count, SPD), axis=1, dtype=jnp.int32)
    slot_index = jnp.arange(capacity, dtype=jnp.int32)
    seq_range = jnp.arange(lengths.shape[0], dtype=jnp.int32)

    def one_device(device, partial_value):
        device = jnp.asarray(device).astype(jnp.int32)
        column_first = (device * capacity).astype(jnp.int32)
        input_rows = lax.dynamic_slice_in_dim(activations, column_first, capacity, 1)
        output_rows = lax.dynamic_slice_in_dim(gradients, column_first, capacity, 1)
        input_projected = project(input_basis, input_rows)
        output_projected = project(output_basis, output_rows)
        left_score = jnp.einsum("dn,kd->nk", output_projected.astype(jnp.float32), left_flat)
        right_score = jnp.einsum("fn,kf->nk", input_projected.astype(jnp.float32), right_flat)
        token_score = jnp.sum((left_score * right_score).reshape(capacity, query_count, rank_count), axis=2)
        row_ends = seq_ends[device]
        seq_slot = jnp.sum((slot_index[:, None] >= row_ends[None, :]).astype(jnp.int32), axis=1)
        position = (device * SPD + jnp.minimum(seq_slot, SPD - 1)).astype(jnp.int32)
        row_ids = jnp.where(seq_slot < SPD, sequence_ids[position], -1).astype(jnp.int32)
        onehot = (seq_range[:, None] == row_ids[None, :]).astype(jnp.float32)
        return partial_value + jnp.dot(onehot, token_score, precision=lax.Precision.HIGHEST, preferred_element_type=jnp.float32)

    initial = jnp.zeros((lengths.shape[0], query_count), jnp.float32)
    return lax.fori_loop(0, device_count, one_device, initial)
```

```python
import jax
import jax.numpy as jnp
from jax import lax
from jax.experimental import pallas as pl
from jax.experimental.pallas import tpu as pltpu
from jax.sharding import PartitionSpec as P

SPD = 8


def project(eigen_basis, feature_rows):
    blocks = eigen_basis.shape[0]
    block_width = eigen_basis.shape[1]
    columns = feature_rows.shape[1]
    shaped = feature_rows.reshape(blocks, block_width, columns)
    mapped = jnp.einsum("bij,bin->bjn", eigen_basis, shaped, preferred_element_type=jnp.float32)
    return mapped.reshape(blocks * block_width, columns).astype(jnp.bfloat16)


def sequence_of(owners, slot_index, lengths, sequence_ids):
    device_count = lengths.shape[0] // SPD
    seq_ends = jnp.cumsum(lengths.reshape(device_count, SPD), axis=1, dtype=jnp.int32)
    row_ends = seq_ends[owners]
    seq_slot = jnp.sum((slot_index[:, None] >= row_ends).astype(jnp.int32), axis=1)
    position = owners * SPD + jnp.minimum(seq_slot, SPD - 1)
    return jnp.where(seq_slot < SPD, sequence_ids[position], -1)


def per_device(
    activations,
    gradients,
    input_basis,
    output_basis,
    query_left,
    query_right,
    lengths,
    sequence_ids,
):
    this_owner = lax.axis_index("seq")
    devices = lax.axis_size("seq")
    capacity = activations.shape[1]
    owners = jnp.full((capacity,), this_owner, jnp.int32)
    slot_index = jnp.arange(capacity, dtype=jnp.int32)
    input_projected = project(input_basis, activations)
    output_projected = project(output_basis, gradients)
    rank_count = query_left.shape[1]
    query_width = query_left.shape[0] * devices * rank_count
    left_piece = lax.all_gather(query_left, "seq", axis=0, tiled=True)
    right_piece = lax.all_gather(query_right, "seq", axis=0, tiled=True)
    flat_count = left_piece.shape[0] * rank_count
    left_part = jnp.einsum(
        "dn,kd->nk",
        output_projected,
        left_piece.reshape(flat_count, left_piece.shape[2]),
        preferred_element_type=jnp.float32,
    )
    right_part = jnp.einsum(
        "fn,kf->nk",
        input_projected,
        right_piece.reshape(flat_count, right_piece.shape[2]),
        preferred_element_type=jnp.float32,
    )
    left_mine, right_mine = (
        lax.psum_scatter(left_part, ("qry", "fac"), scatter_dimension=0, tiled=True),
        lax.psum_scatter(right_part, ("qry", "fac"), scatter_dimension=0, tiled=True),
    )
    rows_mine = left_mine.shape[0]
    token_score = jnp.sum(
        (left_mine * right_mine).reshape(rows_mine, query_width // rank_count, rank_count), axis=2
    )
    row_ids = sequence_of(owners, slot_index, lengths, sequence_ids)
    ids_mine = lax.dynamic_slice_in_dim(
        row_ids, lax.axis_index(("qry", "fac")) * rows_mine, rows_mine
    )
    seq_count = lengths.shape[0]
    onehot = (jnp.arange(seq_count, dtype=jnp.int32)[:, None] == ids_mine[None, :]).astype(
        jnp.float32
    )
    score_term = jnp.dot(
        onehot, token_score, precision=lax.Precision.HIGHEST, preferred_element_type=jnp.float32
    )
    result = lax.psum_scatter(score_term, ("seq", "qry", "fac"), scatter_dimension=0, tiled=True)
    return result


RIGHT_WAVES = 3
TURNS = (1, 2, 3)
DIMS_TN = (((0,), (0,)), ((), ()))
DIMS_NT = (((1,), (1,)), ((), ()))


def fused_kernel(
    len_ref,
    id_ref,
    act_hbm,
    grad_hbm,
    in_basis_hbm,
    out_basis_hbm,
    left_hbm,
    right_hbm,
    out_ref,
    act,
    grad,
    in_basis,
    out_basis,
    q_right,
    q_left,
    right_acc,
    left_acc,
    right_out,
    right_in,
    score_out,
    score_in,
    load_sem,
    own_sem,
    z_send,
    z_recv,
    f_send,
    y_send,
    y_recv,
    s_send,
    s_recv,
    x_send,
    x_recv,
    o_send,
    o_recv,
):
    grp, seq, qry = lax.axis_index("grp"), lax.axis_index("seq"), lax.axis_index("qry")
    z, core = seq // 2, seq % 2
    inner = jnp.logical_or(z == 1, z == 2)
    turn_z = {1: z + 1 - 2 * (z % 2), 2: (z + 2) % 4, 3: 3 - z}
    mesh_id = pl.DeviceIdType.MESH
    y_dev = (1 - grp, seq, qry, 0)
    x_dev = (grp, seq, 1 - qry, 0)
    sib_dev = (grp, z * 2 + 1 - core, qry, 0)
    rank = left_hbm.shape[1]
    in_blocks, in_width = in_basis_hbm.shape[0], in_basis_hbm.shape[1]
    out_blocks, out_width = out_basis_hbm.shape[0], out_basis_hbm.shape[1]
    wave_width = q_right.shape[3]
    left_half = q_left.shape[2]
    waves = RIGHT_WAVES + 1

    def z_dev(t):
        return (grp, turn_z[t] * 2 + core, qry, 0)

    order = []
    for c in range(RIGHT_WAVES):
        half_blocks = in_blocks // 2
        per = half_blocks // RIGHT_WAVES
        order += [(c, "in", h * half_blocks + c * per + k) for h in range(2) for k in range(per)]
    order += [(RIGHT_WAVES, "out", b) for b in range(out_blocks)]

    def loads(i):
        _, kind, b = order[i]
        if kind == "in":
            pairs = ((in_basis_hbm, in_basis, act_hbm, act, in_width),)
        else:
            pairs = ((out_basis_hbm, out_basis, grad_hbm, grad, out_width),)
        basis_src, basis_dst, rows_src, rows_dst, width = pairs[0]
        return (
            pltpu.make_async_copy(basis_src.at[b], basis_dst.at[b], load_sem.at[0, i]),
            pltpu.make_async_copy(
                rows_src.at[pl.ds(b * width, width)],
                rows_dst.at[pl.ds(b * width, width)],
                load_sem.at[1, i],
            ),
        )

    def slot(c, half, query):
        rows = pl.ds(pl.multiple_of(query * rank, rank), rank)
        if c < RIGHT_WAVES:
            return q_right.at[half, c, rows]
        return q_left.at[half, rows]

    def own_piece(c, half):
        if c < RIGHT_WAVES:
            first = half * (wave_width * RIGHT_WAVES) + c * wave_width
            return right_hbm.at[0, :, pl.ds(pl.multiple_of(first, 128), wave_width)]
        first = half * left_half
        return left_hbm.at[0, :, pl.ds(pl.multiple_of(first, 128), left_half)]

    def remote(src, dst, send, recv, dev):
        return pltpu.make_async_remote_copy(
            src_ref=src, dst_ref=dst, send_sem=send, recv_sem=recv,
            device_id=dev, device_id_type=mesh_id,
        )

    def query_of(t):
        return turn_z[t] * 2 + core

    def z_out(c, t):
        return remote(
            own_piece(c, grp), slot(c, grp, seq), z_send.at[t - 1, c], z_recv.at[t - 1, c], z_dev(t)
        )

    def z_in(c, t):
        here = slot(c, grp, query_of(t))
        return remote(here, here, z_send.at[t - 1, c], z_recv.at[t - 1, c], z_dev(t))

    def z_forward(c):
        here = slot(c, grp, query_of(2))
        return remote(here, here, f_send.at[c], z_recv.at[2, c], z_dev(1))

    def y_out(c, t):
        here = slot(c, grp, query_of(t))
        return remote(here, here, y_send.at[t - 1, c], y_recv.at[t - 1, c], y_dev)

    def y_in(c, t):
        here = slot(c, 1 - grp, query_of(t))
        return remote(here, here, y_send.at[t - 1, c], y_recv.at[t - 1, c], y_dev)

    def sib_out(c, t, kind):
        half = grp if kind == 0 else 1 - grp
        if t == 0:
            return remote(
                own_piece(c, half), slot(c, half, seq),
                s_send.at[kind, t, c], s_recv.at[kind, t, c], sib_dev,
            )
        here = slot(c, half, query_of(t))
        return remote(here, here, s_send.at[kind, t, c], s_recv.at[kind, t, c], sib_dev)

    def sib_in(c, t, kind):
        half = grp if kind == 0 else 1 - grp
        source_z = z if t == 0 else turn_z[t]
        here = slot(c, half, source_z * 2 + 1 - core)
        return remote(here, here, s_send.at[kind, t, c], s_recv.at[kind, t, c], sib_dev)

    def own_local(c, half):
        return pltpu.make_async_copy(own_piece(c, half), slot(c, half, seq), own_sem.at[half, c])

    group = 16
    me = seq * 2 + qry

    def peer(o):
        d = (me + o) % group
        return d, (grp, d // 2, d % 2, 0)

    barrier = pltpu.get_barrier_semaphore()
    pl.semaphore_signal(barrier, inc=1, device_id=y_dev, device_id_type=mesh_id)
    for o in range(1, group):
        pl.semaphore_signal(barrier, inc=1, device_id=peer(o)[1], device_id_type=mesh_id)
    for i in range(len(order)):
        for copy in loads(i):
            copy.start()
    for c in range(waves):
        for half in range(2):
            own_local(c, half).start()
    pl.semaphore_wait(barrier, group)

    for c in range(waves):
        for t in (2, 1):
            z_out(c, t).start()

        @pl.when(inner)
        def _():
            z_out(c, 3).start()

        for kind in range(2):
            sib_out(c, 0, kind).start()

    def project(i):
        _, kind, b = order[i]
        for copy in loads(i):
            copy.wait()
        if kind == "in":
            rows = pl.ds(b * in_width, in_width)
            act[rows] = lax.dot_general(
                in_basis[b], act[rows], DIMS_TN, preferred_element_type=jnp.float32
            ).astype(jnp.bfloat16)
        else:
            rows = pl.ds(b * out_width, out_width)
            grad[rows] = lax.dot_general(
                out_basis[b], grad[rows], DIMS_TN, preferred_element_type=jnp.float32
            ).astype(jnp.bfloat16)

    def contract(c):
        for half in range(2):
            own_local(c, half).wait()
        for t in range(4):
            for kind in range(2):
                sib_in(c, t, kind).wait_recv()
        if c < RIGHT_WAVES:
            total = None
            for half in range(2):
                first = half * (wave_width * RIGHT_WAVES) + c * wave_width
                part = jnp.dot(
                    q_right[half, c], act[pl.ds(first, wave_width)],
                    preferred_element_type=jnp.float32,
                )
                total = part if total is None else total + part
            right_acc[...] = total if c == 0 else right_acc[...] + total
        else:
            left_acc[...] = jnp.dot(
                q_left[0], grad[pl.ds(0, left_half)], preferred_element_type=jnp.float32
            ) + jnp.dot(
                q_left[1], grad[pl.ds(left_half, left_half)], preferred_element_type=jnp.float32
            )

    x_copy = remote(right_out, right_in, x_send, x_recv, x_dev)
    steps = [(c, t) for c in range(waves) for t in (2, 1, 3)]
    pending = list(range(len(order)))
    for i, (c, t) in enumerate(steps):
        for _ in range(2):
            if pending:
                project(pending.pop(0))
        z_in(c, t).wait_recv()
        if t == 2:

            @pl.when(inner)
            def _():
                z_forward(c).start()

        y_out(c, t).start()
        sib_out(c, t, 0).start()
        if i >= 1:
            pc, pt = steps[i - 1]
            y_in(pc, pt).wait_recv()
            sib_out(pc, pt, 1).start()
        if c >= 1 and t == 1:
            contract(c - 1)
            if c == RIGHT_WAVES:
                right_out[...] = right_acc[...].astype(jnp.bfloat16)
                x_copy.start()
    pc, pt = steps[-1]
    y_in(pc, pt).wait_recv()
    sib_out(pc, pt, 1).start()
    columns = act.shape[1]
    seq_rows = score_out.shape[0]
    row = lax.broadcasted_iota(jnp.int32, (seq_rows, columns), 0)
    col = lax.broadcasted_iota(jnp.int32, (seq_rows, columns), 1)
    per_out = out_ref.shape[0]
    row_id = jnp.where(row % 8 < per_out, (row // 8) * per_out + row % 8, -1)
    column_id = jnp.full((seq_rows, columns), -2, jnp.int32)
    end = jnp.int32(0)
    for j in range(SPD):
        begin = end
        end = begin + len_ref[seq * SPD + j]
        column_id = jnp.where(
            jnp.logical_and(col >= begin, col < end), id_ref[seq * SPD + j], column_id
        )
    onehot = jnp.where(row_id == column_id, 1.0, 0.0).astype(jnp.float32)
    contract(RIGHT_WAVES)

    x_copy.wait_recv()
    product = left_acc[...] * (right_acc[...] + right_in[...].astype(jnp.float32))
    queries = product.shape[0] // rank
    token = jnp.sum(product.reshape(queries, rank, columns), axis=1)
    token = jnp.concatenate([token, jnp.zeros((128 - queries, columns), jnp.float32)], axis=0)
    score_out[...] = lax.dot_general(
        onehot, token, DIMS_NT,
        precision=lax.Precision.HIGHEST, preferred_element_type=jnp.float32,
    )

    def score_copy(o):
        d, dev = peer(o)
        return remote(
            score_out.at[pl.ds(pl.multiple_of(d * 8, 8), 8)], score_in.at[me],
            o_send.at[o], o_recv.at[o], dev,
        )

    for o in range(1, group):
        score_copy(o).start()
    score_in[me] = score_out[pl.ds(pl.multiple_of(me * 8, 8), 8)]
    for c in range(waves):
        for t in (1, 2):
            z_out(c, t).wait_send()

        @pl.when(inner)
        def _():
            z_out(c, 3).wait_send()
            z_forward(c).wait_send()

        for t in TURNS:
            y_out(c, t).wait_send()
        for t in range(4):
            for kind in range(2):
                sib_out(c, t, kind).wait_send()
    x_copy.wait_send()
    for o in range(1, group):
        d = (me + group - o) % group
        remote(score_in.at[d], score_in.at[d], o_send.at[o], o_recv.at[o], x_dev).wait_recv()
    total = jnp.sum(score_in[...], axis=0)
    out_ref[...] = total[: out_ref.shape[0], : out_ref.shape[1]]
    for o in range(1, group):
        score_copy(o).wait_send()


def fused_device(
    activations,
    gradients,
    input_basis,
    output_basis,
    query_left,
    query_right,
    lengths,
    sequence_ids,
):
    devices = lax.axis_size("seq")
    rank = query_left.shape[1]
    query_rows = query_left.shape[0] * devices * rank
    queries = query_left.shape[0] * devices
    columns = activations.shape[1]
    wave_width = query_right.shape[2] // (2 * RIGHT_WAVES)
    left_half = query_left.shape[2] // 2
    group = devices * lax.axis_size("qry")
    waves = RIGHT_WAVES + 1
    block_count = input_basis.shape[0] + output_basis.shape[0]
    anywhere = pl.BlockSpec(memory_space=pl.ANY)
    scalars = pl.BlockSpec(memory_space=pltpu.SMEM)
    dma = pltpu.SemaphoreType.DMA
    return pl.pallas_call(
        fused_kernel,
        out_shape=jax.ShapeDtypeStruct((lengths.shape[0] // group, queries), jnp.float32),
        in_specs=[scalars, scalars] + [anywhere] * 6,
        out_specs=pl.BlockSpec(memory_space=pltpu.VMEM),
        scratch_shapes=[
            pltpu.VMEM(activations.shape, jnp.bfloat16),
            pltpu.VMEM(gradients.shape, jnp.bfloat16),
            pltpu.VMEM(input_basis.shape, jnp.bfloat16),
            pltpu.VMEM(output_basis.shape, jnp.bfloat16),
            pltpu.VMEM((2, RIGHT_WAVES, query_rows, wave_width), jnp.bfloat16),
            pltpu.VMEM((2, query_rows, left_half), jnp.bfloat16),
            pltpu.VMEM((query_rows, columns), jnp.float32),
            pltpu.VMEM((query_rows, columns), jnp.float32),
            pltpu.VMEM((query_rows, columns), jnp.bfloat16),
            pltpu.VMEM((query_rows, columns), jnp.bfloat16),
            pltpu.VMEM((group * 8, 128), jnp.float32),
            pltpu.VMEM((group, 8, 128), jnp.float32),
            dma((2, block_count)),
            dma((2, waves)),
            dma((3, waves)),
            dma((3, waves)),
            dma((waves,)),
            dma((3, waves)),
            dma((3, waves)),
            dma((2, 4, waves)),
            dma((2, 4, waves)),
            dma,
            dma,
            dma((group,)),
            dma((group,)),
        ],
        compiler_params=pltpu.CompilerParams(
            collective_id=0, has_side_effects=True, vmem_limit_bytes=52 * 1024 * 1024
        ),
    )(
        lengths, sequence_ids, activations, gradients, input_basis, output_basis,
        query_left, query_right,
    )


def solution(mesh):
    sizes = mesh.shape
    fused = (
        sizes["grp"] == 2 and sizes["seq"] == 8 and sizes["qry"] == 2 and sizes["fac"] == 1
    )
    body = fused_device if fused else per_device
    in_specs = (
        P(("qry", "fac"), ("grp", "seq")),
        P(("qry", "fac"), ("grp", "seq")),
        P(("qry", "fac"), None, None),
        P(("qry", "fac"), None, None),
        P("seq", None, ("qry", "fac")),
        P("seq", None, ("qry", "fac")),
        P("grp"),
        P("grp"),
    )
    out_specs = P(("grp", "seq", "qry", "fac"), None)
    return jax.shard_map(
        body, mesh=mesh, in_specs=in_specs, out_specs=out_specs, check_vma=False
    )
```

```python
import jax
import jax.numpy as jnp
from jax import lax
from jax.experimental import pallas as pl
from jax.experimental.pallas import tpu as pltpu
from jax.sharding import PartitionSpec as P

SPD = 8


def project(eigen_basis, feature_rows):
    blocks = eigen_basis.shape[0]
    block_width = eigen_basis.shape[1]
    columns = feature_rows.shape[1]
    shaped = feature_rows.reshape(blocks, block_width, columns)
    mapped = jnp.einsum("bij,bin->bjn", eigen_basis, shaped, preferred_element_type=jnp.float32)
    return mapped.reshape(blocks * block_width, columns).astype(jnp.bfloat16)


def sequence_of(owners, slot_index, lengths, sequence_ids):
    device_count = lengths.shape[0] // SPD
    seq_ends = jnp.cumsum(lengths.reshape(device_count, SPD), axis=1, dtype=jnp.int32)
    row_ends = seq_ends[owners]
    seq_slot = jnp.sum((slot_index[:, None] >= row_ends).astype(jnp.int32), axis=1)
    position = owners * SPD + jnp.minimum(seq_slot, SPD - 1)
    return jnp.where(seq_slot < SPD, sequence_ids[position], -1)


def per_device(
    activations,
    gradients,
    input_basis,
    output_basis,
    query_left,
    query_right,
    lengths,
    sequence_ids,
):
    this_owner = lax.axis_index("seq")
    devices = lax.axis_size("seq")
    capacity = activations.shape[1]
    owners = jnp.full((capacity,), this_owner, jnp.int32)
    slot_index = jnp.arange(capacity, dtype=jnp.int32)
    input_projected = project(input_basis, activations)
    output_projected = project(output_basis, gradients)
    rank_count = query_left.shape[1]
    query_width = query_left.shape[0] * devices * rank_count
    left_piece = lax.all_gather(query_left, "seq", axis=0, tiled=True)
    right_piece = lax.all_gather(query_right, "seq", axis=0, tiled=True)
    flat_count = left_piece.shape[0] * rank_count
    left_part = jnp.einsum(
        "dn,kd->nk",
        output_projected,
        left_piece.reshape(flat_count, left_piece.shape[2]),
        preferred_element_type=jnp.float32,
    )
    right_part = jnp.einsum(
        "fn,kf->nk",
        input_projected,
        right_piece.reshape(flat_count, right_piece.shape[2]),
        preferred_element_type=jnp.float32,
    )
    left_mine, right_mine = (
        lax.psum_scatter(left_part, ("qry", "fac"), scatter_dimension=0, tiled=True),
        lax.psum_scatter(right_part, ("qry", "fac"), scatter_dimension=0, tiled=True),
    )
    rows_mine = left_mine.shape[0]
    token_score = jnp.sum(
        (left_mine * right_mine).reshape(rows_mine, query_width // rank_count, rank_count), axis=2
    )
    row_ids = sequence_of(owners, slot_index, lengths, sequence_ids)
    ids_mine = lax.dynamic_slice_in_dim(
        row_ids, lax.axis_index(("qry", "fac")) * rows_mine, rows_mine
    )
    seq_count = lengths.shape[0]
    onehot = (jnp.arange(seq_count, dtype=jnp.int32)[:, None] == ids_mine[None, :]).astype(
        jnp.float32
    )
    score_term = jnp.dot(
        onehot, token_score, precision=lax.Precision.HIGHEST, preferred_element_type=jnp.float32
    )
    result = lax.psum_scatter(score_term, ("seq", "qry", "fac"), scatter_dimension=0, tiled=True)
    return result


RIGHT_WAVES = 3
TURNS = (1, 2, 3)
AHEAD = 1
LAG = 5
DIMS_TN = (((0,), (0,)), ((), ()))
DIMS_NT = (((1,), (1,)), ((), ()))


def fused_kernel(
    len_ref,
    id_ref,
    act_hbm,
    grad_hbm,
    in_basis_hbm,
    out_basis_hbm,
    left_hbm,
    right_hbm,
    out_ref,
    act,
    grad,
    in_basis,
    out_basis,
    q_right,
    q_left,
    right_acc,
    left_acc,
    right_out,
    right_in,
    score_out,
    score_in,
    load_sem,
    own_sem,
    z_send,
    z_recv,
    f_send,
    y_send,
    y_recv,
    s_send,
    s_recv,
    x_send,
    x_recv,
    o_send,
    o_recv,
):
    grp, seq, qry = lax.axis_index("grp"), lax.axis_index("seq"), lax.axis_index("qry")
    z, core = seq // 2, seq % 2
    inner = jnp.logical_or(z == 1, z == 2)
    turn_z = {1: z + 1 - 2 * (z % 2), 2: (z + 2) % 4, 3: 3 - z}
    mesh_id = pl.DeviceIdType.MESH
    y_dev = (1 - grp, seq, qry, 0)
    x_dev = (grp, seq, 1 - qry, 0)
    sib_dev = (grp, z * 2 + 1 - core, qry, 0)
    rank = left_hbm.shape[1]
    in_blocks, in_width = in_basis_hbm.shape[0], in_basis_hbm.shape[1]
    out_blocks, out_width = out_basis_hbm.shape[0], out_basis_hbm.shape[1]
    wave_width = q_right.shape[3]
    left_half = q_left.shape[2]
    waves = RIGHT_WAVES + 1

    def z_dev(t):
        return (grp, turn_z[t] * 2 + core, qry, 0)

    order = []
    for c in range(RIGHT_WAVES):
        half_blocks = in_blocks // 2
        per = half_blocks // RIGHT_WAVES
        order += [(c, "in", h * half_blocks + c * per + k) for h in range(2) for k in range(per)]
    order += [(RIGHT_WAVES, "out", b) for b in range(out_blocks)]

    def loads(i):
        _, kind, b = order[i]
        if kind == "in":
            pairs = ((in_basis_hbm, in_basis, act_hbm, act, in_width),)
        else:
            pairs = ((out_basis_hbm, out_basis, grad_hbm, grad, out_width),)
        basis_src, basis_dst, rows_src, rows_dst, width = pairs[0]
        return (
            pltpu.make_async_copy(basis_src.at[b], basis_dst.at[b], load_sem.at[0, i]),
            pltpu.make_async_copy(
                rows_src.at[pl.ds(b * width, width)],
                rows_dst.at[pl.ds(b * width, width)],
                load_sem.at[1, i],
            ),
        )

    def slot(c, half, query):
        rows = pl.ds(pl.multiple_of(query * rank, rank), rank)
        if c < RIGHT_WAVES:
            return q_right.at[half, c, rows]
        return q_left.at[half, rows]

    def own_piece(c, half):
        if c < RIGHT_WAVES:
            first = half * (wave_width * RIGHT_WAVES) + c * wave_width
            return right_hbm.at[0, :, pl.ds(pl.multiple_of(first, 128), wave_width)]
        first = half * left_half
        return left_hbm.at[0, :, pl.ds(pl.multiple_of(first, 128), left_half)]

    def remote(src, dst, send, recv, dev):
        return pltpu.make_async_remote_copy(
            src_ref=src, dst_ref=dst, send_sem=send, recv_sem=recv,
            device_id=dev, device_id_type=mesh_id,
        )

    def query_of(t):
        return turn_z[t] * 2 + core

    def z_out(c, t):
        return remote(
            own_piece(c, grp), slot(c, grp, seq), z_send.at[t - 1, c], z_recv.at[t - 1, c], z_dev(t)
        )

    def z_in(c, t):
        here = slot(c, grp, query_of(t))
        return remote(here, here, z_send.at[t - 1, c], z_recv.at[t - 1, c], z_dev(t))

    def z_forward(c):
        here = slot(c, grp, query_of(2))
        return remote(here, here, f_send.at[c], z_recv.at[2, c], z_dev(1))

    def y_out(c, t):
        here = slot(c, grp, query_of(t))
        return remote(here, here, y_send.at[t - 1, c], y_recv.at[t - 1, c], y_dev)

    def y_in(c, t):
        here = slot(c, 1 - grp, query_of(t))
        return remote(here, here, y_send.at[t - 1, c], y_recv.at[t - 1, c], y_dev)

    def sib_out(c, t, kind):
        half = grp if kind == 0 else 1 - grp
        if t == 0:
            return remote(
                own_piece(c, half), slot(c, half, seq),
                s_send.at[kind, t, c], s_recv.at[kind, t, c], sib_dev,
            )
        here = slot(c, half, query_of(t))
        return remote(here, here, s_send.at[kind, t, c], s_recv.at[kind, t, c], sib_dev)

    def sib_in(c, t, kind):
        half = grp if kind == 0 else 1 - grp
        source_z = z if t == 0 else turn_z[t]
        here = slot(c, half, source_z * 2 + 1 - core)
        return remote(here, here, s_send.at[kind, t, c], s_recv.at[kind, t, c], sib_dev)

    def own_local(c, half):
        return pltpu.make_async_copy(own_piece(c, half), slot(c, half, seq), own_sem.at[half, c])

    plane = [sib_dev, x_dev, (grp, z * 2 + 1 - core, 1 - qry, 0)]
    column = [z_dev(t) for t in TURNS]

    barrier = pltpu.get_barrier_semaphore()
    greeted = plane + column + [y_dev]
    for dev in greeted:
        pl.semaphore_signal(barrier, inc=1, device_id=dev, device_id_type=mesh_id)
    for i in range(len(order)):
        for copy in loads(i):
            copy.start()
    for c in range(waves):
        for half in range(2):
            own_local(c, half).start()
    pl.semaphore_wait(barrier, len(greeted))

    def send_wave(c):
        for t in (2, 1):
            z_out(c, t).start()

        @pl.when(inner)
        def _():
            z_out(c, 3).start()

    for c in range(min(AHEAD, waves)):
        send_wave(c)
    for c in range(waves):
        for kind in range(2):
            sib_out(c, 0, kind).start()

    def project(i):
        _, kind, b = order[i]
        for copy in loads(i):
            copy.wait()
        if kind == "in":
            rows = pl.ds(b * in_width, in_width)
            act[rows] = lax.dot_general(
                in_basis[b], act[rows], DIMS_TN, preferred_element_type=jnp.float32
            ).astype(jnp.bfloat16)
        else:
            rows = pl.ds(b * out_width, out_width)
            grad[rows] = lax.dot_general(
                out_basis[b], grad[rows], DIMS_TN, preferred_element_type=jnp.float32
            ).astype(jnp.bfloat16)

    def contract(c):
        for half in range(2):
            own_local(c, half).wait()
        for t in range(4):
            for kind in range(2):
                sib_in(c, t, kind).wait_recv()
        if c < RIGHT_WAVES:
            total = None
            for half in range(2):
                first = half * (wave_width * RIGHT_WAVES) + c * wave_width
                part = jnp.dot(
                    q_right[half, c], act[pl.ds(first, wave_width)],
                    preferred_element_type=jnp.float32,
                )
                total = part if total is None else total + part
            right_acc[...] = total if c == 0 else right_acc[...] + total
        else:
            left_acc[...] = jnp.dot(
                q_left[0], grad[pl.ds(0, left_half)], preferred_element_type=jnp.float32
            ) + jnp.dot(
                q_left[1], grad[pl.ds(left_half, left_half)], preferred_element_type=jnp.float32
            )

    x_copy = remote(right_out, right_in, x_send, x_recv, x_dev)
    steps = [(c, t) for c in range(waves) for t in (2, 1, 3)]
    pending = list(range(len(order)))
    for i in range(len(steps) + LAG):
        if i < len(steps):
            c, t = steps[i]
            for _ in range(2):
                if pending:
                    project(pending.pop(0))
            z_in(c, t).wait_recv()
            if t == 2:

                @pl.when(inner)
                def _():
                    z_forward(c).start()

            y_out(c, t).start()
            if t == 2 and c + AHEAD < waves:
                send_wave(c + AHEAD)
            sib_out(c, t, 0).start()
        if i >= LAG:
            c, t = steps[i - LAG]
            y_in(c, t).wait_recv()
            sib_out(c, t, 1).start()
            if t == 3 and c < RIGHT_WAVES:
                contract(c)
                if c == RIGHT_WAVES - 1:
                    right_out[...] = right_acc[...].astype(jnp.bfloat16)
                    x_copy.start()
    columns = act.shape[1]
    lanes = score_out.shape[2]
    row = lax.broadcasted_iota(jnp.int32, (lanes, columns), 0)
    col = lax.broadcasted_iota(jnp.int32, (lanes, columns), 1)
    column_id = jnp.full((lanes, columns), -1, jnp.int32)
    end = jnp.int32(0)
    for j in range(SPD):
        begin = end
        end = begin + len_ref[seq * SPD + j]
        column_id = jnp.where(
            jnp.logical_and(col >= begin, col < end), id_ref[seq * SPD + j], column_id
        )
    onehot = jnp.where(row == column_id, 1.0, 0.0).astype(jnp.float32)
    contract(RIGHT_WAVES)

    x_copy.wait_recv()
    product = left_acc[...] * (right_acc[...] + right_in[...].astype(jnp.float32))
    queries = product.shape[0] // rank
    token = jnp.sum(product.reshape(queries, rank, columns), axis=1)
    score_out[0] = lax.dot_general(
        token, onehot, DIMS_NT,
        precision=lax.Precision.HIGHEST, preferred_element_type=jnp.float32,
    )

    def score_copy(stage, k):
        return remote(
            score_out.at[stage], score_in.at[stage, k], o_send.at[stage, k], o_recv.at[stage, k],
            (plane, column)[stage][k],
        )

    for k in range(3):
        score_copy(0, k).start()
    for k in range(3):
        score_copy(0, k).wait_recv()
    score_out[1] = (score_out[0] + score_in[0, 0]) + (score_in[0, 1] + score_in[0, 2])
    for k in range(3):
        score_copy(1, k).start()
    for c in range(waves):
        for t in (1, 2):
            z_out(c, t).wait_send()

        @pl.when(inner)
        def _():
            z_out(c, 3).wait_send()
            z_forward(c).wait_send()

        for t in TURNS:
            y_out(c, t).wait_send()
        for t in range(4):
            for kind in range(2):
                sib_out(c, t, kind).wait_send()
    x_copy.wait_send()
    for k in range(3):
        score_copy(1, k).wait_recv()
    total = (score_out[1] + score_in[1, 0]) + (score_in[1, 1] + score_in[1, 2])
    per_out = out_ref.shape[0]
    first_id = (seq * 2 + qry) * per_out
    pick_row = lax.broadcasted_iota(jnp.int32, (8, lanes), 0)
    pick_lane = lax.broadcasted_iota(jnp.int32, (8, lanes), 1)
    pick = jnp.where(pick_lane == pick_row + first_id, 1.0, 0.0).astype(jnp.float32)
    mine = lax.dot_general(
        pick, total, DIMS_NT,
        precision=lax.Precision.HIGHEST, preferred_element_type=jnp.float32,
    )
    out_ref[...] = mine[:per_out]
    for stage in range(2):
        for k in range(3):
            score_copy(stage, k).wait_send()


def fused_device(
    activations,
    gradients,
    input_basis,
    output_basis,
    query_left,
    query_right,
    lengths,
    sequence_ids,
):
    devices = lax.axis_size("seq")
    rank = query_left.shape[1]
    query_rows = query_left.shape[0] * devices * rank
    queries = query_left.shape[0] * devices
    columns = activations.shape[1]
    wave_width = query_right.shape[2] // (2 * RIGHT_WAVES)
    left_half = query_left.shape[2] // 2
    group = devices * lax.axis_size("qry")
    waves = RIGHT_WAVES + 1
    block_count = input_basis.shape[0] + output_basis.shape[0]
    anywhere = pl.BlockSpec(memory_space=pl.ANY)
    scalars = pl.BlockSpec(memory_space=pltpu.SMEM)
    dma = pltpu.SemaphoreType.DMA
    return pl.pallas_call(
        fused_kernel,
        out_shape=jax.ShapeDtypeStruct((lengths.shape[0] // group, queries), jnp.float32),
        in_specs=[scalars, scalars] + [anywhere] * 6,
        out_specs=pl.BlockSpec(memory_space=pltpu.VMEM),
        scratch_shapes=[
            pltpu.VMEM(activations.shape, jnp.bfloat16),
            pltpu.VMEM(gradients.shape, jnp.bfloat16),
            pltpu.VMEM(input_basis.shape, jnp.bfloat16),
            pltpu.VMEM(output_basis.shape, jnp.bfloat16),
            pltpu.VMEM((2, RIGHT_WAVES, query_rows, wave_width), jnp.bfloat16),
            pltpu.VMEM((2, query_rows, left_half), jnp.bfloat16),
            pltpu.VMEM((query_rows, columns), jnp.float32),
            pltpu.VMEM((query_rows, columns), jnp.float32),
            pltpu.VMEM((query_rows, columns), jnp.bfloat16),
            pltpu.VMEM((query_rows, columns), jnp.bfloat16),
            pltpu.VMEM((2, queries, 128), jnp.float32),
            pltpu.VMEM((2, 3, queries, 128), jnp.float32),
            dma((2, block_count)),
            dma((2, waves)),
            dma((3, waves)),
            dma((3, waves)),
            dma((waves,)),
            dma((3, waves)),
            dma((3, waves)),
            dma((2, 4, waves)),
            dma((2, 4, waves)),
            dma,
            dma,
            dma((2, 3)),
            dma((2, 3)),
        ],
        compiler_params=pltpu.CompilerParams(
            collective_id=0, has_side_effects=True, vmem_limit_bytes=62 * 1024 * 1024
        ),
    )(
        lengths, sequence_ids, activations, gradients, input_basis, output_basis,
        query_left, query_right,
    )


def solution(mesh):
    sizes = mesh.shape
    fused = (
        sizes["grp"] == 2 and sizes["seq"] == 8 and sizes["qry"] == 2 and sizes["fac"] == 1
    )
    body = fused_device if fused else per_device
    in_specs = (
        P(("qry", "fac"), ("grp", "seq")),
        P(("qry", "fac"), ("grp", "seq")),
        P(("qry", "fac"), None, None),
        P(("qry", "fac"), None, None),
        P("seq", None, ("qry", "fac")),
        P("seq", None, ("qry", "fac")),
        P("grp"),
        P("grp"),
    )
    out_specs = P(("grp", "seq", "qry", "fac"), None)
    return jax.shard_map(
        body, mesh=mesh, in_specs=in_specs, out_specs=out_specs, check_vma=False
    )
```

```python
import jax
import jax.numpy as jnp
from jax import lax
from jax.experimental import pallas as pl
from jax.experimental.pallas import tpu as pltpu
from jax.sharding import PartitionSpec as P

SPD = 8


def project(eigen_basis, feature_rows):
    blocks = eigen_basis.shape[0]
    block_width = eigen_basis.shape[1]
    columns = feature_rows.shape[1]
    shaped = feature_rows.reshape(blocks, block_width, columns)
    mapped = jnp.einsum("bij,bin->bjn", eigen_basis, shaped, preferred_element_type=jnp.float32)
    return mapped.reshape(blocks * block_width, columns).astype(jnp.bfloat16)


def sequence_of(owners, slot_index, lengths, sequence_ids):
    device_count = lengths.shape[0] // SPD
    seq_ends = jnp.cumsum(lengths.reshape(device_count, SPD), axis=1, dtype=jnp.int32)
    row_ends = seq_ends[owners]
    seq_slot = jnp.sum((slot_index[:, None] >= row_ends).astype(jnp.int32), axis=1)
    position = owners * SPD + jnp.minimum(seq_slot, SPD - 1)
    return jnp.where(seq_slot < SPD, sequence_ids[position], -1)


def per_device(
    activations,
    gradients,
    input_basis,
    output_basis,
    query_left,
    query_right,
    lengths,
    sequence_ids,
):
    this_owner = lax.axis_index("seq")
    devices = lax.axis_size("seq")
    capacity = activations.shape[1]
    owners = jnp.full((capacity,), this_owner, jnp.int32)
    slot_index = jnp.arange(capacity, dtype=jnp.int32)
    input_projected = project(input_basis, activations)
    output_projected = project(output_basis, gradients)
    rank_count = query_left.shape[1]
    query_width = query_left.shape[0] * devices * rank_count
    left_piece = lax.all_gather(query_left, "seq", axis=0, tiled=True)
    right_piece = lax.all_gather(query_right, "seq", axis=0, tiled=True)
    flat_count = left_piece.shape[0] * rank_count
    left_part = jnp.einsum(
        "dn,kd->nk",
        output_projected,
        left_piece.reshape(flat_count, left_piece.shape[2]),
        preferred_element_type=jnp.float32,
    )
    right_part = jnp.einsum(
        "fn,kf->nk",
        input_projected,
        right_piece.reshape(flat_count, right_piece.shape[2]),
        preferred_element_type=jnp.float32,
    )
    left_mine, right_mine = (
        lax.psum_scatter(left_part, ("qry", "fac"), scatter_dimension=0, tiled=True),
        lax.psum_scatter(right_part, ("qry", "fac"), scatter_dimension=0, tiled=True),
    )
    rows_mine = left_mine.shape[0]
    token_score = jnp.sum(
        (left_mine * right_mine).reshape(rows_mine, query_width // rank_count, rank_count), axis=2
    )
    row_ids = sequence_of(owners, slot_index, lengths, sequence_ids)
    ids_mine = lax.dynamic_slice_in_dim(
        row_ids, lax.axis_index(("qry", "fac")) * rows_mine, rows_mine
    )
    seq_count = lengths.shape[0]
    onehot = (jnp.arange(seq_count, dtype=jnp.int32)[:, None] == ids_mine[None, :]).astype(
        jnp.float32
    )
    score_term = jnp.dot(
        onehot, token_score, precision=lax.Precision.HIGHEST, preferred_element_type=jnp.float32
    )
    result = lax.psum_scatter(score_term, ("seq", "qry", "fac"), scatter_dimension=0, tiled=True)
    return result


RIGHT_WAVES = 3
LEFT_WAVES = 1
TURNS = (1, 2, 3)
AHEAD = 1
LAG = 5
DIMS_TN = (((0,), (0,)), ((), ()))
DIMS_NT = (((1,), (1,)), ((), ()))


def fused_kernel(
    len_ref,
    id_ref,
    act_hbm,
    grad_hbm,
    in_basis_hbm,
    out_basis_hbm,
    left_hbm,
    right_hbm,
    out_ref,
    act,
    grad,
    in_basis,
    out_basis,
    q_right,
    q_left,
    right_acc,
    left_acc,
    right_out,
    right_in,
    score_out,
    score_in,
    load_sem,
    own_sem,
    z_send,
    z_recv,
    f_send,
    y_send,
    y_recv,
    s_send,
    s_recv,
    x_send,
    x_recv,
    o_send,
    o_recv,
):
    grp, seq, qry = lax.axis_index("grp"), lax.axis_index("seq"), lax.axis_index("qry")
    z, core = seq // 2, seq % 2
    inner = jnp.logical_or(z == 1, z == 2)
    turn_z = {1: z + 1 - 2 * (z % 2), 2: (z + 2) % 4, 3: 3 - z}
    mesh_id = pl.DeviceIdType.MESH
    y_dev = (1 - grp, seq, qry, 0)
    x_dev = (grp, seq, 1 - qry, 0)
    sib_dev = (grp, z * 2 + 1 - core, qry, 0)
    rank = left_hbm.shape[1]
    in_blocks, in_width = in_basis_hbm.shape[0], in_basis_hbm.shape[1]
    out_blocks, out_width = out_basis_hbm.shape[0], out_basis_hbm.shape[1]
    wave_width = q_right.shape[3]
    left_width = q_left.shape[3]
    waves = RIGHT_WAVES + LEFT_WAVES

    def z_dev(t):
        return (grp, turn_z[t] * 2 + core, qry, 0)

    order = []
    for c in range(RIGHT_WAVES):
        half_blocks = in_blocks // 2
        per = half_blocks // RIGHT_WAVES
        order += [(c, "in", h * half_blocks + c * per + k) for h in range(2) for k in range(per)]
    order += [(RIGHT_WAVES, "out", b) for b in range(out_blocks)]

    def loads(i):
        _, kind, b = order[i]
        if kind == "in":
            pairs = ((in_basis_hbm, in_basis, act_hbm, act, in_width),)
        else:
            pairs = ((out_basis_hbm, out_basis, grad_hbm, grad, out_width),)
        basis_src, basis_dst, rows_src, rows_dst, width = pairs[0]
        return (
            pltpu.make_async_copy(basis_src.at[b], basis_dst.at[b], load_sem.at[0, i]),
            pltpu.make_async_copy(
                rows_src.at[pl.ds(b * width, width)],
                rows_dst.at[pl.ds(b * width, width)],
                load_sem.at[1, i],
            ),
        )

    def slot(c, half, query):
        rows = pl.ds(pl.multiple_of(query * rank, rank), rank)
        if c < RIGHT_WAVES:
            return q_right.at[half, c, rows]
        return q_left.at[half, c - RIGHT_WAVES, rows]

    def own_piece(c, half):
        if c < RIGHT_WAVES:
            first = half * (wave_width * RIGHT_WAVES) + c * wave_width
            return right_hbm.at[0, :, pl.ds(pl.multiple_of(first, 128), wave_width)]
        first = half * (left_width * LEFT_WAVES) + (c - RIGHT_WAVES) * left_width
        return left_hbm.at[0, :, pl.ds(pl.multiple_of(first, 128), left_width)]

    def remote(src, dst, send, recv, dev):
        return pltpu.make_async_remote_copy(
            src_ref=src, dst_ref=dst, send_sem=send, recv_sem=recv,
            device_id=dev, device_id_type=mesh_id,
        )

    def query_of(t):
        return turn_z[t] * 2 + core

    def z_out(c, t):
        return remote(
            own_piece(c, grp), slot(c, grp, seq), z_send.at[t - 1, c], z_recv.at[t - 1, c], z_dev(t)
        )

    def z_in(c, t):
        here = slot(c, grp, query_of(t))
        return remote(here, here, z_send.at[t - 1, c], z_recv.at[t - 1, c], z_dev(t))

    def z_forward(c):
        here = slot(c, grp, query_of(2))
        return remote(here, here, f_send.at[c], z_recv.at[2, c], z_dev(1))

    def y_out(c, t):
        here = slot(c, grp, query_of(t))
        return remote(here, here, y_send.at[t - 1, c], y_recv.at[t - 1, c], y_dev)

    def y_in(c, t):
        here = slot(c, 1 - grp, query_of(t))
        return remote(here, here, y_send.at[t - 1, c], y_recv.at[t - 1, c], y_dev)

    def sib_out(c, t, kind):
        half = grp if kind == 0 else 1 - grp
        if t == 0:
            return remote(
                own_piece(c, half), slot(c, half, seq),
                s_send.at[kind, t, c], s_recv.at[kind, t, c], sib_dev,
            )
        here = slot(c, half, query_of(t))
        return remote(here, here, s_send.at[kind, t, c], s_recv.at[kind, t, c], sib_dev)

    def sib_in(c, t, kind):
        half = grp if kind == 0 else 1 - grp
        source_z = z if t == 0 else turn_z[t]
        here = slot(c, half, source_z * 2 + 1 - core)
        return remote(here, here, s_send.at[kind, t, c], s_recv.at[kind, t, c], sib_dev)

    def own_local(c, half):
        return pltpu.make_async_copy(own_piece(c, half), slot(c, half, seq), own_sem.at[half, c])

    plane = [sib_dev, x_dev, (grp, z * 2 + 1 - core, 1 - qry, 0)]
    column = [z_dev(t) for t in TURNS]
    far = [(grp, turn_z[t] * 2 + e, q, 0) for t in TURNS for e, q in
           ((1 - core, qry), (core, 1 - qry), (1 - core, 1 - qry))]
    others = plane + column + far

    barrier = pltpu.get_barrier_semaphore()
    greeted = others + [y_dev]
    for dev in greeted:
        pl.semaphore_signal(barrier, inc=1, device_id=dev, device_id_type=mesh_id)
    for i in range(len(order)):
        for copy in loads(i):
            copy.start()
    for c in range(waves):
        for half in range(2):
            own_local(c, half).start()
    pl.semaphore_wait(barrier, len(greeted))

    def send_wave(c):
        for t in (2, 1):
            z_out(c, t).start()

        @pl.when(inner)
        def _():
            z_out(c, 3).start()

    for c in range(min(AHEAD, waves)):
        send_wave(c)
    for c in range(waves):
        for kind in range(2):
            sib_out(c, 0, kind).start()

    def project(i):
        _, kind, b = order[i]
        for copy in loads(i):
            copy.wait()
        if kind == "in":
            rows = pl.ds(b * in_width, in_width)
            act[rows] = lax.dot_general(
                in_basis[b], act[rows], DIMS_TN, preferred_element_type=jnp.float32
            ).astype(jnp.bfloat16)
        else:
            rows = pl.ds(b * out_width, out_width)
            grad[rows] = lax.dot_general(
                out_basis[b], grad[rows], DIMS_TN, preferred_element_type=jnp.float32
            ).astype(jnp.bfloat16)

    def contract(c):
        for half in range(2):
            own_local(c, half).wait()
        for t in range(4):
            for kind in range(2):
                sib_in(c, t, kind).wait_recv()
        if c < RIGHT_WAVES:
            total = None
            for half in range(2):
                first = half * (wave_width * RIGHT_WAVES) + c * wave_width
                part = jnp.dot(
                    q_right[half, c], act[pl.ds(first, wave_width)],
                    preferred_element_type=jnp.float32,
                )
                total = part if total is None else total + part
            right_acc[...] = total if c == 0 else right_acc[...] + total
        else:
            k = c - RIGHT_WAVES
            total = None
            for half in range(2):
                first = half * (left_width * LEFT_WAVES) + k * left_width
                part = jnp.dot(
                    q_left[half, k], grad[pl.ds(first, left_width)],
                    preferred_element_type=jnp.float32,
                )
                total = part if total is None else total + part
            left_acc[...] = total if k == 0 else left_acc[...] + total

    x_copy = remote(right_out, right_in, x_send, x_recv, x_dev)
    steps = [(c, t) for c in range(waves) for t in (2, 1, 3)]
    pending = list(range(len(order)))
    for i in range(len(steps) + LAG):
        if i < len(steps):
            c, t = steps[i]
            for _ in range(2):
                if pending:
                    project(pending.pop(0))
            z_in(c, t).wait_recv()
            if t == 2:

                @pl.when(inner)
                def _():
                    z_forward(c).start()

            y_out(c, t).start()
            if t == 2 and c + AHEAD < waves:
                send_wave(c + AHEAD)
            sib_out(c, t, 0).start()
        if i >= LAG:
            c, t = steps[i - LAG]
            y_in(c, t).wait_recv()
            sib_out(c, t, 1).start()
            if t == 3 and c < waves - 1:
                contract(c)
                if c == RIGHT_WAVES - 1:
                    right_out[...] = right_acc[...].astype(jnp.bfloat16)
                    x_copy.start()
    columns = act.shape[1]
    lanes = score_out.shape[1]
    row = lax.broadcasted_iota(jnp.int32, (lanes, columns), 0)
    col = lax.broadcasted_iota(jnp.int32, (lanes, columns), 1)
    column_id = jnp.full((lanes, columns), -1, jnp.int32)
    end = jnp.int32(0)
    for j in range(SPD):
        begin = end
        end = begin + len_ref[seq * SPD + j]
        column_id = jnp.where(
            jnp.logical_and(col >= begin, col < end), id_ref[seq * SPD + j], column_id
        )
    onehot = jnp.where(row == column_id, 1.0, 0.0).astype(jnp.float32)
    contract(waves - 1)

    x_copy.wait_recv()
    product = left_acc[...] * (right_acc[...] + right_in[...].astype(jnp.float32))
    queries = product.shape[0] // rank
    token = jnp.sum(product.reshape(queries, rank, columns), axis=1)
    score_out[...] = lax.dot_general(
        token, onehot, DIMS_NT,
        precision=lax.Precision.HIGHEST, preferred_element_type=jnp.float32,
    )

    def score_copy(k):
        return remote(score_out, score_in.at[k], o_send.at[k], o_recv.at[k], others[k])

    for k in range(len(others)):
        score_copy(k).start()
    for c in range(waves):
        for t in (1, 2):
            z_out(c, t).wait_send()

        @pl.when(inner)
        def _():
            z_out(c, 3).wait_send()
            z_forward(c).wait_send()

        for t in TURNS:
            y_out(c, t).wait_send()
        for t in range(4):
            for kind in range(2):
                sib_out(c, t, kind).wait_send()
    x_copy.wait_send()
    for k in range(len(others)):
        score_copy(k).wait_recv()
    total = score_out[...] + jnp.sum(score_in[...], axis=0)
    per_out = out_ref.shape[0]
    first_id = (seq * 2 + qry) * per_out
    pick_row = lax.broadcasted_iota(jnp.int32, (8, lanes), 0)
    pick_lane = lax.broadcasted_iota(jnp.int32, (8, lanes), 1)
    pick = jnp.where(pick_lane == pick_row + first_id, 1.0, 0.0).astype(jnp.float32)
    mine = lax.dot_general(
        pick, total, DIMS_NT,
        precision=lax.Precision.HIGHEST, preferred_element_type=jnp.float32,
    )
    out_ref[...] = mine[:per_out]
    for k in range(len(others)):
        score_copy(k).wait_send()


def fused_device(
    activations,
    gradients,
    input_basis,
    output_basis,
    query_left,
    query_right,
    lengths,
    sequence_ids,
):
    devices = lax.axis_size("seq")
    rank = query_left.shape[1]
    query_rows = query_left.shape[0] * devices * rank
    queries = query_left.shape[0] * devices
    columns = activations.shape[1]
    wave_width = query_right.shape[2] // (2 * RIGHT_WAVES)
    left_width = query_left.shape[2] // (2 * LEFT_WAVES)
    group = devices * lax.axis_size("qry")
    waves = RIGHT_WAVES + LEFT_WAVES
    block_count = input_basis.shape[0] + output_basis.shape[0]
    anywhere = pl.BlockSpec(memory_space=pl.ANY)
    scalars = pl.BlockSpec(memory_space=pltpu.SMEM)
    dma = pltpu.SemaphoreType.DMA
    return pl.pallas_call(
        fused_kernel,
        out_shape=jax.ShapeDtypeStruct((lengths.shape[0] // group, queries), jnp.float32),
        in_specs=[scalars, scalars] + [anywhere] * 6,
        out_specs=pl.BlockSpec(memory_space=pltpu.VMEM),
        scratch_shapes=[
            pltpu.VMEM(activations.shape, jnp.bfloat16),
            pltpu.VMEM(gradients.shape, jnp.bfloat16),
            pltpu.VMEM(input_basis.shape, jnp.bfloat16),
            pltpu.VMEM(output_basis.shape, jnp.bfloat16),
            pltpu.VMEM((2, RIGHT_WAVES, query_rows, wave_width), jnp.bfloat16),
            pltpu.VMEM((2, LEFT_WAVES, query_rows, left_width), jnp.bfloat16),
            pltpu.VMEM((query_rows, columns), jnp.float32),
            pltpu.VMEM((query_rows, columns), jnp.float32),
            pltpu.VMEM((query_rows, columns), jnp.bfloat16),
            pltpu.VMEM((query_rows, columns), jnp.bfloat16),
            pltpu.VMEM((queries, 128), jnp.float32),
            pltpu.VMEM((group - 1, queries, 128), jnp.float32),
            dma((2, block_count)),
            dma((2, waves)),
            dma((3, waves)),
            dma((3, waves)),
            dma((waves,)),
            dma((3, waves)),
            dma((3, waves)),
            dma((2, 4, waves)),
            dma((2, 4, waves)),
            dma,
            dma,
            dma((group - 1,)),
            dma((group - 1,)),
        ],
        compiler_params=pltpu.CompilerParams(
            collective_id=0, has_side_effects=True, vmem_limit_bytes=62 * 1024 * 1024
        ),
    )(
        lengths, sequence_ids, activations, gradients, input_basis, output_basis,
        query_left, query_right,
    )


def solution(mesh):
    sizes = mesh.shape
    fused = (
        sizes["grp"] == 2 and sizes["seq"] == 8 and sizes["qry"] == 2 and sizes["fac"] == 1
    )
    body = fused_device if fused else per_device
    in_specs = (
        P(("qry", "fac"), ("grp", "seq")),
        P(("qry", "fac"), ("grp", "seq")),
        P(("qry", "fac"), None, None),
        P(("qry", "fac"), None, None),
        P("seq", None, ("qry", "fac")),
        P("seq", None, ("qry", "fac")),
        P("grp"),
        P("grp"),
    )
    out_specs = P(("grp", "seq", "qry", "fac"), None)
    return jax.shard_map(
        body, mesh=mesh, in_specs=in_specs, out_specs=out_specs, check_vma=False
    )
```
